32 devices in a mesh: lon: 8 (over z, y), lat: 4 (over x, core).
Axes of the slice: x: 2, y: 2, z: 4, core: 2. Of those that a mesh axis runs over, the one named last changes fastest.
Arguments:
- ocean_state: float32 [4, 6, 768, 1024], P(None, None, 'lat', 'lon'), may hold values from -4 to 4
- sea_mask: int32 [6, 768, 1024], P(None, 'lat', 'lon'), may hold values 0 or 1
Outputs:
- new_state: float32 [4, 6, 768, 1024], P(None, None, 'lat', 'lon')
The draws below stay inside these ranges and needn't reach their ends.
All inputs are finite; a program needn't handle non-finite values. No bound on the sum of `sea_mask` on one device may be relied on, other than what follows from the above.
Results may differ from the reference program's by a relative error of at most 0.00002.
Values sent between devices are 32-bit elements; how exact they have to be, the bound alone decides.
A program may use at most 128 MiB of HBM per device.

```python
import jax
import jax.numpy as jnp
from jax import lax

LEV = 6
STEPS = 2
NLAT = 768
NLON = 1024


def place_ends(drawn, rng, low, top_value):
    shape = drawn.shape
    place = [jax.random.randint(jax.random.fold_in(rng, axis), (), 0, shape[axis]) for axis in range(len(shape))]
    drawn = drawn.at[tuple(place)].set(low)
    longest = shape.index(max(shape))
    place[longest] = (place[longest] + 1) % shape[longest]
    return drawn.at[tuple(place)].set(top_value)


def level_of(key, shape, split, low, largest):
    def one(axis_at, shards_of):
        steps = jax.random.uniform(jax.random.fold_in(jax.random.fold_in(key, 6), axis_at), (shards_of,), jnp.float32, low / len(split), largest / len(split))
        return jnp.repeat(jnp.exp(steps), shape[axis_at] // shards_of).reshape((-1,) + (1,) * (len(shape) - axis_at - 1))

    loudness = one(*split[0])
    for cut in split[1:]:
        loudness = loudness * one(*cut)
    return loudness


def gaussian(own_key, extent, deviation, most, shards=(), dtype=jnp.bfloat16):
    loudness = level_of(own_key, extent, shards, -0.22, 0.18) if shards else 1.0
    values = jax.random.normal(own_key, extent, jnp.float32) * deviation * loudness
    return jnp.minimum(jnp.maximum(values, -most), most).astype(dtype)


def setup_inputs(seed: int = 0) -> dict:
    streams_of = jax.random.split(jax.random.key(seed), 3)
    return {
        "ocean_state": gaussian(streams_of[0], (4, LEV, NLAT, NLON), 1.0, 4.0, ((2, 4), (3, 8)), jnp.float32),
        "sea_mask": place_ends((jax.random.randint(streams_of[1], (LEV, NLAT, NLON), 0, 8) < 7).astype(jnp.int32), jax.random.fold_in(streams_of[1], 1), 0, 1),
    }


time_step = 0.1
thermal_coef = 0.2
haline_coef = 0.8
gravity = 0.5
spreading_coefficient = 0.05
viscosity = 0.05
coriolis_base = -0.6
coriolis_slope = 1.2


def east_diff(field):
    centre = field[..., 2:-2, :]
    return (8.0 * (centre[..., 3:-1] - centre[..., 1:-3]) - (centre[..., 4:] - centre[..., :-4])) / 12.0


def north_diff(field):
    centre = field[..., 2:-2]
    return (8.0 * (centre[..., 3:-1, :] - centre[..., 1:-3, :]) - (centre[..., 4:, :] - centre[..., :-4, :])) / 12.0


def second_derivative_sum(field):
    centre = field[..., 2:-2, 2:-2]
    return field[..., 3:-1, 2:-2] + field[..., 1:-3, 2:-2] + field[..., 2:-2, 3:-1] + field[..., 2:-2, 1:-3] - 4.0 * centre


def level_tendency(bordered_grid_values, pressure, coriolis, water_indicator):
    heat_distribution, brine_concentration, eastward_current, northward_current = bordered_grid_values[0], bordered_grid_values[1], bordered_grid_values[2], bordered_grid_values[3]
    u_centre = eastward_current[..., 2:-2, 2:-2]
    v_centre = northward_current[..., 2:-2, 2:-2]

    def kept_prior_values(field):
        return -(u_centre * east_diff(field) + v_centre * north_diff(field))

    heat_increment = kept_prior_values(heat_distribution) + spreading_coefficient * second_derivative_sum(heat_distribution)
    brine_increment = kept_prior_values(brine_concentration) + spreading_coefficient * second_derivative_sum(brine_concentration)
    eastward_gradient = kept_prior_values(eastward_current) + coriolis * v_centre - east_diff(pressure) + viscosity * second_derivative_sum(eastward_current)
    northward_gradient = kept_prior_values(northward_current) - coriolis * u_centre - north_diff(pressure) + viscosity * second_derivative_sum(northward_current)
    return jnp.stack([heat_increment, brine_increment, eastward_gradient, northward_gradient]) * water_indicator


def fold_signs():
    return jnp.array([1.0, 1.0, -1.0, -1.0], jnp.float32)[:, None, None, None]


def extend_global(fields):
    widened = jnp.concatenate([fields[..., -2:], fields, fields[..., :2]], axis=-1)
    ghost = widened[..., -2:, :][..., ::-1, ::-1] * fold_signs()
    bottom = jnp.zeros_like(ghost)
    return jnp.concatenate([bottom, widened, ghost], axis=-2)


def tendency(fields, coriolis, water_indicator):
    bordered_grid_values = extend_global(fields)
    density = haline_coef * bordered_grid_values[1] - thermal_coef * bordered_grid_values[0]
    pressure = gravity * jnp.cumsum(density, axis=0)

    def one_level(items):
        level_fields, level_pressure, level_wet = items
        return level_tendency(level_fields, level_pressure, coriolis, level_wet)

    result = lax.map(one_level, (jnp.moveaxis(bordered_grid_values, 1, 0), pressure, water_indicator))
    return jnp.moveaxis(result, 0, 1)


def reference(ocean_state, sea_mask):
    water_indicator = sea_mask.astype(jnp.float32)
    rows = jnp.arange(NLAT).astype(jnp.float32)
    coriolis = (coriolis_base + coriolis_slope * (rows + 0.5) / NLAT)[:, None]
    fields = ocean_state * water_indicator
    for repeat in range(STEPS):
        first = fields + time_step * tendency(fields, coriolis, water_indicator)
        second = 0.75 * fields + 0.25 * (first + time_step * tendency(first, coriolis, water_indicator))
        fields = fields / 3.0 + (2.0 / 3.0) * (second + time_step * tendency(second, coriolis, water_indicator))
    return fields
```

```python
import functools

import jax
import jax.numpy as jnp
from jax import lax
from jax.experimental import pallas as pl
from jax.experimental.pallas import tpu as pltpu
from jax.sharding import PartitionSpec as P

STEPS = 2
SUB = 8
LANE = 128
FIELDS = 4
CHUNK = 2

time_step = 0.1
thermal_coef = 0.2
haline_coef = 0.8
gravity = 0.5
spreading_coefficient = 0.05
coriolis_base = -0.6
coriolis_slope = 1.2

MESH = pl.DeviceIdType.MESH


def kernel(
    levels, rows, width, lon_n, lat_n,
    in_hbm, mask_hbm, out_hbm,
    fin, min_, fout, wet, q0, q1, q2,
    lon_out, lon_in, lat_out, lat_in,
    local_sem, lon_ssem, lon_rsem, lat_ssem, lat_rsem,
):
    items = FIELDS * levels
    run = rows // SUB
    positions = run // 2
    chunks = positions // CHUNK
    tiles = width // LANE
    lon = lax.axis_index("lon")
    lat = lax.axis_index("lat")
    east = lax.rem(lon + 1, lon_n)
    west = lax.rem(lon + lon_n - 1, lon_n)
    mirror = lon_n - 1 - lon

    loads = []
    for j in range(tiles):
        lanes = pl.ds(j * LANE, LANE)
        loads.append(pltpu.make_async_copy(mask_hbm.at[:, :, lanes], min_.at[j], local_sem.at[2 * j]))
        loads.append(pltpu.make_async_copy(in_hbm.at[:, :, :, lanes], fin.at[j], local_sem.at[2 * j + 1]))
    for copy in loads:
        copy.start()

    barrier = pltpu.get_barrier_semaphore()
    pl.semaphore_signal(barrier, inc=1, device_id={"lon": east}, device_id_type=MESH)
    pl.semaphore_signal(barrier, inc=1, device_id={"lon": west}, device_id_type=MESH)

    @pl.when(lat > 0)
    def _():
        pl.semaphore_signal(barrier, inc=1, device_id={"lat": lat - 1}, device_id_type=MESH)

    @pl.when(lat < lat_n - 1)
    def _():
        pl.semaphore_signal(barrier, inc=1, device_id={"lat": lat + 1}, device_id_type=MESH)

    @pl.when(lat == lat_n - 1)
    def _():
        pl.semaphore_signal(barrier, inc=1, device_id={"lon": mirror}, device_id_type=MESH)

    @pl.when(lat == 0)
    def _():
        lat_in[0] = jnp.zeros(lat_in.shape[1:], jnp.float32)
        pl.semaphore_wait(barrier, 3)

    @pl.when(lat > 0)
    def _():
        pl.semaphore_wait(barrier, 4)

    for copy in loads:
        copy.wait()

    lane = lax.broadcasted_iota(jnp.int32, (SUB, LANE), 1)
    wide_lane = lax.broadcasted_iota(jnp.int32, (SUB, width), 1)
    sub = lax.broadcasted_iota(jnp.int32, (SUB, width), 0)
    slot_of = lane // 4
    early = lax.rem(lane, 4) < 2
    row_base = (lat * rows).astype(jnp.float32) + (sub * run).astype(jnp.float32) + 0.5
    total = rows * lat_n
    cor_base = coriolis_base + row_base * (coriolis_slope / total)

    def rolled(value, shift):
        return pltpu.roll(value, shift % value.shape[1], 1)

    def place(packed, value, i):
        return jnp.where(slot_of == i, rolled(value, 2 + 4 * i)[:, :LANE], packed)

    def unplace(packed, i):
        edge = rolled(packed, LANE - 2 - 4 * i)
        return edge if tiles == 1 else jnp.concatenate([edge] * tiles, axis=1)

    def pair_of(j):
        return lax.rem(j + positions - 1, positions)

    def keep_edges(n, j, first, second):
        lon_out[0, n, j] = jnp.where(early, first, rolled(second, 2))
        lon_out[1, n, j] = jnp.where(early, rolled(first, -2), second)

    def lon_copy(d, n, c):
        part = pl.ds(c * CHUNK, CHUNK)
        return pltpu.make_async_remote_copy(
            src_ref=lon_out.at[d, n, part], dst_ref=lon_in.at[d, n, part],
            send_sem=lon_ssem.at[d, n, c], recv_sem=lon_rsem.at[d, n, c],
            device_id={"lon": east if d == 0 else west}, device_id_type=MESH)

    def lat_copy(src, dst, n, where):
        return pltpu.make_async_remote_copy(
            src_ref=lat_out.at[src, n], dst_ref=lat_in.at[dst, n],
            send_sem=lat_ssem.at[src, n], recv_sem=lat_rsem.at[dst, n],
            device_id=where, device_id_type=MESH)

    def send_lat(n, q):
        for i in range(items):
            for k in range(2):
                lat_out[1, n, pl.ds(2 * i + k, 1)] = q[i, 2 + k, pl.ds(0, 1)]

        @pl.when(lat > 0)
        def _():
            lat_copy(1, 1, n, {"lat": lat - 1}).start()

        @pl.when(lat < lat_n - 1)
        def _():
            for i in range(items):
                for k in range(2):
                    lat_out[0, n, pl.ds(2 * i + k, 1)] = q[i, run + k, pl.ds(SUB - 1, 1)]
            lat_copy(0, 0, n, {"lat": lat + 1}).start()

        @pl.when(lat == lat_n - 1)
        def _():
            for i in range(items):
                for k in range(2):
                    lat_out[0, n, pl.ds(2 * i + k, 1)] = q[i, run + 1 - k, pl.ds(SUB - 1, 1)]
            back = (
                lax.broadcasted_iota(jnp.int32, (width, width), 0)
                + lax.broadcasted_iota(jnp.int32, (width, width), 1)
            ) == width - 1
            line = lax.broadcasted_iota(jnp.int32, (2 * items, width), 0)
            turned = jnp.dot(
                lat_out[0, n], back.astype(jnp.float32),
                precision=lax.Precision.HIGHEST, preferred_element_type=jnp.float32)
            lat_out[0, n] = jnp.where(line < items, turned, -turned)
            lat_copy(0, 1, n, {"lon": mirror}).start()

    def send_chunk(n, c, q):
        lon_copy(0, n, c).start()
        lon_copy(1, n, c).start()

        @pl.when(c == 0)
        def _():
            send_lat(n, q)

    def first_state(c, carry):
        def one(jj, inner):
            j = c * CHUNK + jj
            p = pair_of(j)
            packs = []
            for a in range(2):
                r = 2 * p + a
                packed = jnp.zeros((SUB, LANE), jnp.float32)
                for lv in range(levels):
                    w = [min_[t, lv, pl.ds(r, SUB, stride=run)].astype(jnp.float32) for t in range(tiles)]
                    w = jnp.concatenate(w, axis=1) if tiles > 1 else w[0]
                    wet[lv, r] = w
                    for f in range(FIELDS):
                        i = f * levels + lv
                        x = [fin[t, f, lv, pl.ds(r, SUB, stride=run)] for t in range(tiles)]
                        x = (jnp.concatenate(x, axis=1) if tiles > 1 else x[0]) * w
                        q0[i, r + 2] = x
                        packed = place(packed, x, i)
                packs.append(packed)
            keep_edges(0, j, *packs)
            return inner

        lax.fori_loop(0, CHUNK, one, 0)
        send_chunk(0, c, q0)
        return carry

    lax.fori_loop(0, chunks, first_state, 0)

    def stage(n, qi, qb, qo, base_coef, in_coef, step_coef, last):
        @pl.when(lat > 0)
        def _():
            lat_copy(0, 0, n, {"lat": lat - 1}).wait_recv()

        lat_copy(0, 1, n, {"lon": mirror}).wait_recv()
        for i in range(items):
            for k in range(2):
                south = jnp.broadcast_to(lat_in[0, n, pl.ds(2 * i + k, 1)], (SUB, width))
                north = jnp.broadcast_to(lat_in[1, n, pl.ds(2 * i + k, 1)], (SUB, width))
                qi[i, k] = jnp.where(sub == 0, south, pltpu.roll(qi[i, run + k], 1, 0))
                qi[i, run + 2 + k] = jnp.where(sub == SUB - 1, north, pltpu.roll(qi[i, 2 + k], SUB - 1, 0))

        own = in_coef - 4.0 * spreading_coefficient * step_coef

        def one_row(r, halo):
            cor = cor_base + r.astype(jnp.float32) * (coriolis_slope / total)
            grad_x = jnp.zeros((SUB, width), jnp.float32)
            grad_y = jnp.zeros((SUB, width), jnp.float32)
            packed = jnp.zeros((SUB, LANE), jnp.float32)
            for lv in range(levels):
                gain = wet[lv, r] * step_coef
                u = qi[2 * levels + lv, r + 2]
                v = qi[3 * levels + lv, r + 2]
                un = u * (-1.0 / 12.0)
                vn = v * (-1.0 / 12.0)
                slopes = []
                for f in range(FIELDS):
                    i = f * levels + lv
                    x = qi[i, r + 2]
                    s2, s1, n1, n2 = qi[i, r], qi[i, r + 1], qi[i, r + 3], qi[i, r + 4]
                    edge = unplace(halo, i)
                    w1 = rolled(jnp.where(wide_lane == width - 1, edge, x), 1)
                    w2 = rolled(jnp.where(wide_lane >= width - 2, edge, x), 2)
                    e1 = rolled(jnp.where(wide_lane == 0, edge, x), -1)
                    e2 = rolled(jnp.where(wide_lane <= 1, edge, x), -2)
                    dx = 8.0 * (e1 - w1) - (e2 - w2)
                    dy = 8.0 * (n1 - s1) - (n2 - s2)
                    change = un * dx + vn * dy + spreading_coefficient * ((e1 + w1) + (n1 + s1))
                    slopes.append((dx, dy))
                    if f == 2:
                        kr = gravity * haline_coef / 12.0
                        kt = gravity * thermal_coef / 12.0
                        grad_x = grad_x + (kr * slopes[1][0] - kt * slopes[0][0])
                        grad_y = grad_y + (kr * slopes[1][1] - kt * slopes[0][1])
                        change = change + (cor * v - grad_x)
                    if f == 3:
                        change = change - (cor * u + grad_y)
                    new = own * x + gain * change
                    if base_coef:
                        new = new + base_coef * qb[i, r + 2]
                    if last:
                        for t in range(tiles):
                            fout[t, f, lv, pl.ds(r, SUB, stride=run)] = new[:, t * LANE:(t + 1) * LANE]
                    else:
                        qo[i, r + 2] = new
                        packed = place(packed, new, i)
            return packed

        def chunk(c, carry):
            lon_copy(0, n, c).wait_recv()
            lon_copy(1, n, c).wait_recv()

            def one(jj, inner):
                j = c * CHUNK + jj
                p = pair_of(j)
                from_west = lon_in[0, n, j]
                from_east = lon_in[1, n, j]
                first = one_row(2 * p, jnp.where(early, from_west, rolled(from_east, 2)))
                second = one_row(2 * p + 1, jnp.where(early, rolled(from_west, -2), from_east))
                if not last:
                    keep_edges(n + 1, j, first, second)
                return inner

            lax.fori_loop(0, CHUNK, one, 0)
            if not last:
                send_chunk(n + 1, c, qo)
            return carry

        lax.fori_loop(0, chunks, chunk, 0)

    for step in range(STEPS):
        n = 3 * step
        stage(n, q0, None, q1, 0.0, 1.0, time_step, False)
        stage(n + 1, q1, q0, q2, 0.75, 0.25, 0.25 * time_step, False)
        stage(n + 2, q2, q0, q0, 1.0 / 3.0, 2.0 / 3.0, 2.0 / 3.0 * time_step, step == STEPS - 1)

    stores = []
    for j in range(tiles):
        stores.append(pltpu.make_async_copy(
            fout.at[j], out_hbm.at[:, :, :, pl.ds(j * LANE, LANE)], local_sem.at[2 * j]))
    for copy in stores:
        copy.start()

    def sent(k, carry):
        n = k // chunks
        c = lax.rem(k, chunks)
        lon_copy(0, n, c).wait_send()
        lon_copy(1, n, c).wait_send()
        return carry

    lax.fori_loop(0, 3 * STEPS * chunks, sent, 0)
    for n in range(3 * STEPS):
        lat_copy(0, 1, n, {"lon": mirror}).wait_send()

        @pl.when(lat > 0)
        def _():
            lat_copy(1, 1, n, {"lat": lat - 1}).wait_send()

    for copy in stores:
        copy.wait()


def shards(lon_n, lat_n, ocean_state, sea_mask):
    fields, levels, rows, width = ocean_state.shape
    items = fields * levels
    run = rows // SUB
    tiles = width // LANE
    stages = 3 * STEPS
    positions = run // 2
    chunks = positions // CHUNK
    f32 = jnp.float32
    state = pltpu.VMEM((items, run + 4, SUB, width), f32)
    return pl.pallas_call(
        functools.partial(kernel, levels, rows, width, lon_n, lat_n),
        out_shape=jax.ShapeDtypeStruct(ocean_state.shape, f32),
        in_specs=[pl.BlockSpec(memory_space=pl.ANY)] * 2,
        out_specs=pl.BlockSpec(memory_space=pl.ANY),
        scratch_shapes=[
            pltpu.VMEM((tiles, fields, levels, rows, LANE), f32),
            pltpu.VMEM((tiles, levels, rows, LANE), jnp.int32),
            pltpu.VMEM((tiles, fields, levels, rows, LANE), f32),
            pltpu.VMEM((levels, run, SUB, width), f32),
            state, state, state,
            pltpu.VMEM((2, stages, positions, SUB, LANE), f32),
            pltpu.VMEM((2, stages, positions, SUB, LANE), f32),
            pltpu.VMEM((2, stages, 2 * items, width), f32),
            pltpu.VMEM((2, stages, 2 * items, width), f32),
            pltpu.SemaphoreType.DMA((2 * tiles,)),
            pltpu.SemaphoreType.DMA((2, stages, chunks)),
            pltpu.SemaphoreType.DMA((2, stages, chunks)),
            pltpu.SemaphoreType.DMA((2, stages)),
            pltpu.SemaphoreType.DMA((2, stages)),
        ],
        compiler_params=pltpu.CompilerParams(
            collective_id=0, has_side_effects=True, vmem_limit_bytes=56 * 2**20),
    )(ocean_state, sea_mask)


def solution(mesh):
    in_specs = (P(None, None, "lat", "lon"), P(None, "lat", "lon"))
    out_specs = P(None, None, "lat", "lon")
    body = functools.partial(shards, mesh.shape["lon"], mesh.shape["lat"])
    return jax.shard_map(body, mesh=mesh, in_specs=in_specs, out_specs=out_specs, check_vma=False)
```

```python
import functools

import jax
import jax.numpy as jnp
from jax import lax
from jax.experimental import pallas as pl
from jax.experimental.pallas import tpu as pltpu
from jax.sharding import PartitionSpec as P

STEPS = 2
SUB = 8
LANE = 128
FIELDS = 4
CHUNK = 2

time_step = 0.1
thermal_coef = 0.2
haline_coef = 0.8
gravity = 0.5
spreading_coefficient = 0.05
coriolis_base = -0.6
coriolis_slope = 1.2

MESH = pl.DeviceIdType.MESH


def kernel(
    levels, rows, width, lon_n, lat_n,
    in_hbm, mask_hbm, out_hbm,
    fin, min_, fout, wet, q0, q1, q2,
    weight, edge_weight, only, left, edge_left, found,
    lon_out, lon_in, lat_out, lat_in,
    local_sem, lon_ssem, lon_rsem, lat_ssem, lat_rsem,
):
    items = FIELDS * levels
    run = rows // SUB
    positions = run // 2
    chunks = positions // CHUNK
    tiles = width // LANE
    lon = lax.axis_index("lon")
    lat = lax.axis_index("lat")
    east = lax.rem(lon + 1, lon_n)
    west = lax.rem(lon + lon_n - 1, lon_n)
    mirror = lon_n - 1 - lon

    loads = []
    for j in range(tiles):
        lanes = pl.ds(j * LANE, LANE)
        loads.append(pltpu.make_async_copy(mask_hbm.at[:, :, lanes], min_.at[j], local_sem.at[2 * j]))
        loads.append(pltpu.make_async_copy(in_hbm.at[:, :, :, lanes], fin.at[j], local_sem.at[2 * j + 1]))
    for copy in loads:
        copy.start()

    barrier = pltpu.get_barrier_semaphore()
    pl.semaphore_signal(barrier, inc=1, device_id={"lon": east}, device_id_type=MESH)
    pl.semaphore_signal(barrier, inc=1, device_id={"lon": west}, device_id_type=MESH)

    @pl.when(lat > 0)
    def _():
        pl.semaphore_signal(barrier, inc=1, device_id={"lat": lat - 1}, device_id_type=MESH)

    @pl.when(lat < lat_n - 1)
    def _():
        pl.semaphore_signal(barrier, inc=1, device_id={"lat": lat + 1}, device_id_type=MESH)

    @pl.when(lat == lat_n - 1)
    def _():
        pl.semaphore_signal(barrier, inc=1, device_id={"lon": mirror}, device_id_type=MESH)

    @pl.when(lat == 0)
    def _():
        lat_in[0] = jnp.zeros(lat_in.shape[1:], jnp.float32)
        pl.semaphore_wait(barrier, 3)

    @pl.when(lat > 0)
    def _():
        pl.semaphore_wait(barrier, 4)

    for copy in loads:
        copy.wait()

    lane = lax.broadcasted_iota(jnp.int32, (SUB, LANE), 1)
    sub = lax.broadcasted_iota(jnp.int32, (SUB, width), 0)
    slot_of = lane // 4
    early = lax.rem(lane, 4) < 2
    row_base = (lat * rows).astype(jnp.float32) + (sub * run).astype(jnp.float32) + 0.5
    total = rows * lat_n
    cor_base = coriolis_base + row_base * (coriolis_slope / total)

    def rolled(value, shift):
        return pltpu.roll(value, shift % value.shape[1], 1)

    def place(packed, value, i):
        return jnp.where(slot_of == i, rolled(value, 2 + 4 * i)[:, :LANE], packed)

    def taps(source, shape):
        column = lax.broadcasted_iota(jnp.int32, shape, 1)
        d = source - lax.rem(column, width)

        def at(k):
            return (d == k).astype(jnp.float32)

        return jnp.where(
            column < width, 8.0 * (at(1) - at(-1)) - (at(2) - at(-2)), at(1) + at(-1)
        ).astype(jnp.bfloat16)

    shape = (2 * width, 2 * width)
    weight[...] = taps(lax.rem(lax.broadcasted_iota(jnp.int32, shape, 0), width), shape)
    shape = (2 * LANE, 2 * width)
    line = lax.rem(lax.broadcasted_iota(jnp.int32, shape, 0), 4)
    edge_weight[...] = taps(jnp.where(line < 2, line - 2, line - 2 + width), shape)
    slot_two = lax.broadcasted_iota(jnp.int32, (2 * SUB, LANE), 1) // 4
    for i in range(items):
        only[i] = (slot_two == i).astype(jnp.float32).astype(jnp.bfloat16)

    def split(value):
        high = value.astype(jnp.bfloat16)
        return high, (value - high.astype(jnp.float32)).astype(jnp.bfloat16)

    def pair_of(j):
        return lax.rem(j + positions - 1, positions)

    def keep_edges(n, j, first, second):
        lon_out[0, n, j] = jnp.where(early, first, rolled(second, 2))
        lon_out[1, n, j] = jnp.where(early, rolled(first, -2), second)

    def lon_copy(d, n, c):
        part = pl.ds(c * CHUNK, CHUNK)
        return pltpu.make_async_remote_copy(
            src_ref=lon_out.at[d, n, part], dst_ref=lon_in.at[d, n, part],
            send_sem=lon_ssem.at[d, n, c], recv_sem=lon_rsem.at[d, n, c],
            device_id={"lon": east if d == 0 else west}, device_id_type=MESH)

    def lat_copy(src, dst, n, where):
        return pltpu.make_async_remote_copy(
            src_ref=lat_out.at[src, n], dst_ref=lat_in.at[dst, n],
            send_sem=lat_ssem.at[src, n], recv_sem=lat_rsem.at[dst, n],
            device_id=where, device_id_type=MESH)

    def send_lat(n, q):
        for i in range(items):
            for k in range(2):
                lat_out[1, n, pl.ds(2 * i + k, 1)] = q[i, 2 + k, pl.ds(0, 1)]

        @pl.when(lat > 0)
        def _():
            lat_copy(1, 1, n, {"lat": lat - 1}).start()

        @pl.when(lat < lat_n - 1)
        def _():
            for i in range(items):
                for k in range(2):
                    lat_out[0, n, pl.ds(2 * i + k, 1)] = q[i, run + k, pl.ds(SUB - 1, 1)]
            lat_copy(0, 0, n, {"lat": lat + 1}).start()

        @pl.when(lat == lat_n - 1)
        def _():
            for i in range(items):
                for k in range(2):
                    lat_out[0, n, pl.ds(2 * i + k, 1)] = q[i, run + 1 - k, pl.ds(SUB - 1, 1)]
            back = (
                lax.broadcasted_iota(jnp.int32, (width, width), 0)
                + lax.broadcasted_iota(jnp.int32, (width, width), 1)
            ) == width - 1
            line = lax.broadcasted_iota(jnp.int32, (2 * items, width), 0)
            turned = jnp.dot(
                lat_out[0, n], back.astype(jnp.float32),
                precision=lax.Precision.HIGHEST, preferred_element_type=jnp.float32)
            lat_out[0, n] = jnp.where(line < items, turned, -turned)
            lat_copy(0, 1, n, {"lon": mirror}).start()

    def send_chunk(n, c, q):
        lon_copy(0, n, c).start()
        lon_copy(1, n, c).start()

        @pl.when(c == 0)
        def _():
            send_lat(n, q)

    def first_state(c, carry):
        def one(jj, inner):
            j = c * CHUNK + jj
            p = pair_of(j)
            packs = []
            for a in range(2):
                r = 2 * p + a
                packed = jnp.zeros((SUB, LANE), jnp.float32)
                for lv in range(levels):
                    w = [min_[t, lv, pl.ds(r, SUB, stride=run)].astype(jnp.float32) for t in range(tiles)]
                    w = jnp.concatenate(w, axis=1) if tiles > 1 else w[0]
                    wet[lv, r] = w
                    for f in range(FIELDS):
                        i = f * levels + lv
                        x = [fin[t, f, lv, pl.ds(r, SUB, stride=run)] for t in range(tiles)]
                        x = (jnp.concatenate(x, axis=1) if tiles > 1 else x[0]) * w
                        q0[i, r + 2] = x
                        packed = place(packed, x, i)
                packs.append(packed)
            keep_edges(0, j, *packs)
            return inner

        lax.fori_loop(0, CHUNK, one, 0)
        send_chunk(0, c, q0)
        return carry

    lax.fori_loop(0, chunks, first_state, 0)

    def stage(n, qi, qb, qo, base_coef, in_coef, step_coef, last):
        @pl.when(lat > 0)
        def _():
            lat_copy(0, 0, n, {"lat": lat - 1}).wait_recv()

        lat_copy(0, 1, n, {"lon": mirror}).wait_recv()
        for i in range(items):
            for k in range(2):
                south = jnp.broadcast_to(lat_in[0, n, pl.ds(2 * i + k, 1)], (SUB, width))
                north = jnp.broadcast_to(lat_in[1, n, pl.ds(2 * i + k, 1)], (SUB, width))
                qi[i, k] = jnp.where(sub == 0, south, pltpu.roll(qi[i, run + k], 1, 0))
                qi[i, run + 2 + k] = jnp.where(sub == SUB - 1, north, pltpu.roll(qi[i, 2 + k], SUB - 1, 0))

        own = in_coef - 4.0 * spreading_coefficient * step_coef

        def one_row(r, a):
            cor = cor_base + r.astype(jnp.float32) * (coriolis_slope / total)
            grad_x = jnp.zeros((SUB, width), jnp.float32)
            grad_y = jnp.zeros((SUB, width), jnp.float32)
            packed = jnp.zeros((SUB, LANE), jnp.float32)
            for lv in range(levels):
                gain = wet[lv, r] * step_coef
                u = qi[2 * levels + lv, r + 2]
                v = qi[3 * levels + lv, r + 2]
                un = u * (-1.0 / 12.0)
                vn = v * (-1.0 / 12.0)
                slopes = []
                for f in range(FIELDS):
                    i = f * levels + lv
                    x = qi[i, r + 2]
                    s2, s1, n1, n2 = qi[i, r], qi[i, r + 1], qi[i, r + 3], qi[i, r + 4]
                    line = pl.ds(i * 2 * SUB + a * SUB, SUB)
                    dx = found[line, pl.ds(0, width)]
                    sides = found[line, pl.ds(width, width)]
                    dy = 8.0 * (n1 - s1) - (n2 - s2)
                    change = un * dx + vn * dy + spreading_coefficient * (sides + (n1 + s1))
                    slopes.append((dx, dy))
                    if f == 2:
                        kr = gravity * haline_coef / 12.0
                        kt = gravity * thermal_coef / 12.0
                        grad_x = grad_x + (kr * slopes[1][0] - kt * slopes[0][0])
                        grad_y = grad_y + (kr * slopes[1][1] - kt * slopes[0][1])
                        change = change + (cor * v - grad_x)
                    if f == 3:
                        change = change - (cor * u + grad_y)
                    new = own * x + gain * change
                    if base_coef:
                        new = new + base_coef * qb[i, r + 2]
                    if last:
                        for t in range(tiles):
                            fout[t, f, lv, pl.ds(r, SUB, stride=run)] = new[:, t * LANE:(t + 1) * LANE]
                    else:
                        qo[i, r + 2] = new
                        packed = place(packed, new, i)
            return packed

        def chunk(c, carry):
            lon_copy(0, n, c).wait_recv()
            lon_copy(1, n, c).wait_recv()

            def one(jj, inner):
                j = c * CHUNK + jj
                p = pair_of(j)
                from_west = lon_in[0, n, j]
                from_east = lon_in[1, n, j]
                halo = jnp.concatenate([
                    jnp.where(early, from_west, rolled(from_east, 2)),
                    jnp.where(early, rolled(from_west, -2), from_east)], axis=0)
                halo_high, halo_low = split(halo)
                for i in range(items):
                    lines = pl.ds(i * 2 * SUB, 2 * SUB)
                    high, low = split(qi[i, pl.ds(2 * p + 2, 2)].reshape(2 * SUB, width))
                    left[lines, pl.ds(0, width)] = high
                    left[lines, pl.ds(width, width)] = low
                    edge_left[lines, pl.ds(0, LANE)] = halo_high * only[i]
                    edge_left[lines, pl.ds(LANE, LANE)] = halo_low * only[i]
                found[...] = jnp.dot(
                    left[...], weight[...], preferred_element_type=jnp.float32
                ) + jnp.dot(edge_left[...], edge_weight[...], preferred_element_type=jnp.float32)
                first = one_row(2 * p, 0)
                second = one_row(2 * p + 1, 1)
                if not last:
                    keep_edges(n + 1, j, first, second)
                return inner

            lax.fori_loop(0, CHUNK, one, 0)
            if not last:
                send_chunk(n + 1, c, qo)
            return carry

        lax.fori_loop(0, chunks, chunk, 0)

    for step in range(STEPS):
        n = 3 * step
        stage(n, q0, None, q1, 0.0, 1.0, time_step, False)
        stage(n + 1, q1, q0, q2, 0.75, 0.25, 0.25 * time_step, False)
        stage(n + 2, q2, q0, q0, 1.0 / 3.0, 2.0 / 3.0, 2.0 / 3.0 * time_step, step == STEPS - 1)

    stores = []
    for j in range(tiles):
        stores.append(pltpu.make_async_copy(
            fout.at[j], out_hbm.at[:, :, :, pl.ds(j * LANE, LANE)], local_sem.at[2 * j]))
    for copy in stores:
        copy.start()

    def sent(k, carry):
        n = k // chunks
        c = lax.rem(k, chunks)
        lon_copy(0, n, c).wait_send()
        lon_copy(1, n, c).wait_send()
        return carry

    lax.fori_loop(0, 3 * STEPS * chunks, sent, 0)
    for n in range(3 * STEPS):
        lat_copy(0, 1, n, {"lon": mirror}).wait_send()

        @pl.when(lat > 0)
        def _():
            lat_copy(1, 1, n, {"lat": lat - 1}).wait_send()

    for copy in stores:
        copy.wait()


def shards(lon_n, lat_n, ocean_state, sea_mask):
    fields, levels, rows, width = ocean_state.shape
    items = fields * levels
    run = rows // SUB
    tiles = width // LANE
    stages = 3 * STEPS
    positions = run // 2
    chunks = positions // CHUNK
    f32 = jnp.float32
    state = pltpu.VMEM((items, run + 4, SUB, width), f32)
    return pl.pallas_call(
        functools.partial(kernel, levels, rows, width, lon_n, lat_n),
        out_shape=jax.ShapeDtypeStruct(ocean_state.shape, f32),
        in_specs=[pl.BlockSpec(memory_space=pl.ANY)] * 2,
        out_specs=pl.BlockSpec(memory_space=pl.ANY),
        scratch_shapes=[
            pltpu.VMEM((tiles, fields, levels, rows, LANE), f32),
            pltpu.VMEM((tiles, levels, rows, LANE), jnp.int32),
            pltpu.VMEM((tiles, fields, levels, rows, LANE), f32),
            pltpu.VMEM((levels, run, SUB, width), f32),
            state, state, state,
            pltpu.VMEM((2 * width, 2 * width), jnp.bfloat16),
            pltpu.VMEM((2 * LANE, 2 * width), jnp.bfloat16),
            pltpu.VMEM((items, 2 * SUB, LANE), jnp.bfloat16),
            pltpu.VMEM((items * 2 * SUB, 2 * width), jnp.bfloat16),
            pltpu.VMEM((items * 2 * SUB, 2 * LANE), jnp.bfloat16),
            pltpu.VMEM((items * 2 * SUB, 2 * width), f32),
            pltpu.VMEM((2, stages, positions, SUB, LANE), f32),
            pltpu.VMEM((2, stages, positions, SUB, LANE), f32),
            pltpu.VMEM((2, stages, 2 * items, width), f32),
            pltpu.VMEM((2, stages, 2 * items, width), f32),
            pltpu.SemaphoreType.DMA((2 * tiles,)),
            pltpu.SemaphoreType.DMA((2, stages, chunks)),
            pltpu.SemaphoreType.DMA((2, stages, chunks)),
            pltpu.SemaphoreType.DMA((2, stages)),
            pltpu.SemaphoreType.DMA((2, stages)),
        ],
        compiler_params=pltpu.CompilerParams(
            collective_id=0, has_side_effects=True, vmem_limit_bytes=56 * 2**20),
    )(ocean_state, sea_mask)


def solution(mesh):
    in_specs = (P(None, None, "lat", "lon"), P(None, "lat", "lon"))
    out_specs = P(None, None, "lat", "lon")
    body = functools.partial(shards, mesh.shape["lon"], mesh.shape["lat"])
    return jax.shard_map(body, mesh=mesh, in_specs=in_specs, out_specs=out_specs, check_vma=False)
```
